32 devices in a mesh: groups: 2 (over y), chan: 4 (over z), tm: 4 (over x, core).
Axes of the slice: x: 2, y: 2, z: 4, core: 2. Of those that a mesh axis runs over, the one named last changes fastest.
Arguments:
- raw: bfloat16 [8192, 2048], P(('groups', 'chan'), 'tm'), parts along dimension 0, may hold values from -20 to 20
- send_blocks: int32 [4, 4, 4, 1], P('chan', 'tm'), may hold values from 0 to 1, as said below
- pair_count: int32 [4, 4, 4], P('chan', 'tm'), may hold values from 0 to 1, as said below
Outputs:
- xspec: bfloat16 [8, 4, 4, 1, 2, 2, 128, 128], P(('groups', 'chan'), 'tm'), parts along dimension 0
The draws below stay inside these ranges and needn't reach their ends.
There are 2 independent parts, one for each index of `groups`. The reference program is written for one: setup_inputs(seed, part) draws one part's arguments, and reference() takes and returns one part's arrays. A program takes and returns all parts, laid end to end along the dimension named above; an argument that names none is the same for every part. Nothing has to cross between parts.
Inputs may be any that keep to these rules, and one draw needn't show every extreme that they name: Each list send_blocks[p, t, c, :] names 1 distinct local blocks of device (p, t). pair_count[c, t, c] is 0; pair_count[c, t, p] is 1 where p and c differ by one; in every index t of tm some owner has 1 from every other source.
All inputs are finite; a program needn't handle non-finite values.
Results may differ from the reference program's by a relative error of at most 0.0066.
Values may be sent and summed in bfloat16 or wider, within the bound.
A program may use at most 192 MiB of HBM per device.

```python
import math
import jax
import jax.numpy as jnp
import numpy as np
from jax import lax

BLOCK = 128
NT = 2048
F0 = 128
NBAND = 512
SUBW = 64
RAD = 15
BPD = 2
CAP = 1
NCH = 4096
N_CHAN = 4
N_TM = 4


def draw_raw(key, part):
    keys = jax.random.split(key, 3)
    chan_scale = jnp.exp(jax.random.uniform(keys[0], (NCH, 1), jnp.float32, math.log(0.3), math.log(3.0)))
    time_scale = jnp.exp(jax.random.uniform(keys[1], (1, NT), jnp.float32, math.log(0.5), math.log(2.0)))
    values = jax.random.normal(keys[2], (NCH, NT), jnp.float32) * chan_scale * time_scale
    return jnp.clip(values, -20.0, 20.0).astype(jnp.bfloat16)


def draw_send_blocks(key, part):
    local = jax.random.fold_in(key, 11)
    scores = jax.random.randint(local, (N_CHAN, N_TM, N_CHAN, BPD), 0, 1 << 20)
    scores = scores * BPD + jnp.arange(BPD, dtype=jnp.int32)
    order = jnp.argsort(scores, axis=-1, stable=True).astype(jnp.int32)
    return order[..., :CAP]


def draw_pair_count(key, part):
    local = jax.random.fold_in(key, 12)
    keys = jax.random.split(local, 2)
    owner = jnp.arange(N_CHAN, dtype=jnp.int32)[:, None, None]
    source = jnp.arange(N_CHAN, dtype=jnp.int32)[None, None, :]
    apart = jnp.abs(owner - source)
    base = jax.random.randint(keys[0], (N_CHAN, N_TM, N_CHAN), 0, CAP + 1)
    counts = jnp.where(apart <= max(1, N_CHAN // 4), base, 0)
    counts = jnp.where(apart == 1, CAP, counts)
    heavy = jax.random.randint(keys[1], (N_TM,), 0, N_CHAN)
    counts = jnp.where(owner == heavy[None, :, None], CAP, counts)
    counts = jnp.where(apart == 0, 0, counts)
    return counts.astype(jnp.int32)


def setup_inputs(seed: int = 0, part: int = 0) -> dict:
    key_of = jax.random.split(jax.random.key(seed), 4)
    part_keys = jax.random.split(jax.random.fold_in(key_of[3], part), 4)
    raw = draw_raw(jax.random.fold_in(jax.random.fold_in(key_of[3], part), 71), part)
    send_blocks = draw_send_blocks(jax.random.fold_in(key_of[3], 71), part)
    pair_count = draw_pair_count(jax.random.fold_in(key_of[3], 71), part)
    return dict(raw=raw, send_blocks=send_blocks, pair_count=pair_count)


def sinc_value(arg):
    if arg == 0:
        return 1.0
    return math.sin(math.pi * arg) / (math.pi * arg)

def filter_taps():
    low = F0 / NT
    high = (F0 + NBAND) / NT
    taps = []
    for offset in range(-RAD, RAD + 1):
        value = 2.0 * high * sinc_value(2.0 * high * offset) - 2.0 * low * sinc_value(2.0 * low * offset)
        value = value * (0.5 + 0.5 * math.cos(math.pi * offset / (RAD + 1)))
        taps.append(value)
    return taps

def dft_table():
    samples = np.arange(NT)[:, None]
    freqs = np.arange(F0, F0 + NBAND)[None, :]
    phase = samples * freqs % NT
    angle = 2.0 * np.pi * phase / NT
    return np.concatenate([np.cos(angle), -np.sin(angle)], axis=1)

def band_filter(slab):
    taps = filter_taps()
    signal = slab.astype(jnp.float32)
    total = jnp.zeros(signal.shape, jnp.float32)
    for index in range(2 * RAD + 1):
        total = total + jnp.float32(taps[index]) * jnp.roll(signal, index - RAD, axis=1)
    return total.astype(jnp.bfloat16)

def whiten(spectrum):
    rows = spectrum.shape[0]
    real_part = spectrum[:, :NBAND].reshape(rows, NBAND // SUBW, SUBW)
    imag_part = spectrum[:, NBAND:].reshape(rows, NBAND // SUBW, SUBW)
    power = lax.optimization_barrier(jnp.mean(real_part * real_part + imag_part * imag_part, axis=2, keepdims=True))
    level = 1.0 / jnp.sqrt(power + 1e-06)
    out = jnp.concatenate([(real_part * level).reshape(rows, NBAND), (imag_part * level).reshape(rows, NBAND)], axis=1)
    return out.astype(jnp.bfloat16)

def process(slab):
    table = jnp.asarray(dft_table(), dtype=jnp.bfloat16)
    filtered = band_filter(slab)
    spectrum = jnp.dot(filtered, table, preferred_element_type=jnp.float32)
    return whiten(spectrum).reshape(BPD, BLOCK, 2 * NBAND)

def reference(raw, send_blocks, pair_count):
    slabs = raw.reshape(N_CHAN * N_TM, BPD * BLOCK, NT)
    spectra = lax.map(process, slabs).reshape(N_CHAN, N_TM, BPD, BLOCK, 2 * NBAND)
    sources = jnp.arange(N_CHAN, dtype=jnp.int32)

    def owner(flat):
        chan_idx = flat // N_TM
        time_idx = flat % N_TM
        own = spectra[chan_idx, time_idx].astype(jnp.float32)
        turned = jnp.concatenate([own[..., NBAND:], -own[..., :NBAND]], axis=-1)
        both = jnp.stack([own, turned], axis=1)
        ids = send_blocks[:, time_idx, chan_idx, :]
        picked = spectra[sources[:, None], time_idx, ids].astype(jnp.float32)
        result = jnp.einsum('lrif,pkjf->pklrij', both, picked) * (1.0 / math.sqrt(NBAND))
        live = jnp.arange(CAP, dtype=jnp.int32)[None, :] < pair_count[chan_idx, time_idx][:, None]
        result = jnp.where(live[:, :, None, None, None, None], result, 0.0)
        return result.astype(jnp.bfloat16)
    out = lax.map(owner, jnp.arange(N_CHAN * N_TM, dtype=jnp.int32))
    return out.reshape(N_CHAN, N_TM, N_CHAN, CAP, BPD, 2, BLOCK, BLOCK)
```

```python
import functools
import math

import jax
import jax.numpy as jnp
import numpy as np
from jax import lax
from jax.experimental import pallas as pl
from jax.experimental.pallas import tpu as pltpu
from jax.sharding import PartitionSpec as P

BLOCK = 128
NT = 2048
F0 = 128
NBAND = 512
SUBW = 64
RAD = 15
TILE = 256
SIDE = 128


def sinc_value(arg):
    if arg == 0:
        return 1.0
    return math.sin(math.pi * arg) / (math.pi * arg)


def filter_taps():
    low = F0 / NT
    high = (F0 + NBAND) / NT
    taps = []
    for offset in range(-RAD, RAD + 1):
        value = 2.0 * high * sinc_value(2.0 * high * offset) - 2.0 * low * sinc_value(
            2.0 * low * offset
        )
        value = value * (0.5 + 0.5 * math.cos(math.pi * offset / (RAD + 1)))
        taps.append(value)
    return taps


def dft_table():
    samples = np.arange(NT)[:, None]
    freqs = np.arange(F0, F0 + NBAND)[None, :]
    phase = samples * freqs % NT
    angle = 2.0 * np.pi * phase / NT
    return np.concatenate([np.cos(angle), -np.sin(angle)], axis=1)


def filter_bands():
    taps = np.asarray(filter_taps(), np.float64).astype(np.float32)
    u = np.arange(TILE + 2 * SIDE)[:, None]
    v = np.arange(TILE)[None, :]
    k = v + SIDE - u
    band = np.where(np.abs(k) <= RAD, taps[np.clip(k + RAD, 0, 2 * RAD)], 0).astype(np.float32)
    first = band.astype(jnp.bfloat16)
    second = (band - first.astype(np.float32)).astype(jnp.bfloat16)
    return np.stack([first, second])


def segment_ones():
    run = np.arange(128) // SUBW
    return (run[:, None] == run[None, :]).astype(jnp.bfloat16)


def dot(a, b):
    return jnp.dot(a, b, preferred_element_type=jnp.float32)


def kernel(
    peers,
    teams,
    raw_ref,
    table_ref,
    bands_ref,
    ones_ref,
    send_ref,
    count_ref,
    out_ref,
    rows,
    table,
    filtered,
    paired,
    outbox,
    inbox,
    table_sem,
    own_sem,
    tm_send,
    tm_recv,
    ch_send,
    ch_recv,
):
    c = lax.axis_index("chan")
    t = lax.axis_index("tm")
    blocks = rows.shape[0]
    span = raw_ref.shape[1]

    load_table = pltpu.make_async_copy(table_ref, table, table_sem)
    load_table.start()

    barrier = pltpu.get_barrier_semaphore()
    for o in range(1, teams):
        pl.semaphore_signal(barrier, inc=1, device_id={"tm": lax.rem(t + o, teams)})
    for o in range(1, peers):
        pl.semaphore_signal(barrier, inc=1, device_id={"chan": lax.rem(c + o, peers)})
    pl.semaphore_wait(barrier, teams + peers - 2)

    mine = pl.ds(pl.multiple_of(t * span, 128), span)

    def part(o, l):
        q = lax.rem(t + o, teams)
        start = pl.multiple_of((q * blocks + l) * BLOCK, BLOCK)
        return pltpu.make_async_remote_copy(
            src_ref=raw_ref.at[pl.ds(start, BLOCK), :],
            dst_ref=rows.at[l, :, mine],
            send_sem=tm_send.at[o - 1, l],
            recv_sem=tm_recv.at[o - 1, l],
            device_id={"tm": q},
        )

    def own(l):
        start = pl.multiple_of((t * blocks + l) * BLOCK, BLOCK)
        return pltpu.make_async_copy(
            raw_ref.at[pl.ds(start, BLOCK), :], rows.at[l, :, mine], own_sem.at[l]
        )

    for l in range(blocks):
        for o in range(1, teams):
            part(o, l).start()
        own(l).start()
    load_table.wait()

    def block_step(l, carry):
        own(l).wait()
        for o in range(1, teams):
            part(o, l).wait_recv()
        for j in range(NT // TILE):
            lo, hi = j * TILE - SIDE, (j + 1) * TILE + SIDE
            if lo < 0:
                window = jnp.concatenate([rows[l, :, NT + lo :], rows[l, :, :hi]], axis=1)
            elif hi > NT:
                window = jnp.concatenate([rows[l, :, lo:], rows[l, :, : hi - NT]], axis=1)
            else:
                window = rows[l, :, lo:hi]
            value = dot(window, bands_ref[0]) + dot(window, bands_ref[1])
            filtered[:, j * TILE : (j + 1) * TILE] = value.astype(jnp.bfloat16)
        step = 256
        for f in range(0, NBAND, step):
            real = dot(filtered[...], table[:, f : f + step])
            imag = dot(filtered[...], table[:, NBAND + f : NBAND + f + step])
            power = real * real + imag * imag
            for g in range(0, step, 128):
                p = power[:, g : g + 128]
                first = p.astype(jnp.bfloat16)
                second = (p - first.astype(jnp.float32)).astype(jnp.bfloat16)
                total = dot(first, ones_ref[...]) + dot(second, ones_ref[...])
                level = lax.rsqrt(total * (1.0 / SUBW) + 1e-06)
                re = (real[:, g : g + 128] * level).astype(jnp.bfloat16)
                im = (imag[:, g : g + 128] * level).astype(jnp.bfloat16)
                at = f + g
                paired[l, 0, :, at : at + 128] = re
                paired[l, 0, :, NBAND + at : NBAND + at + 128] = im
                paired[l, 1, :, at : at + 128] = im
                paired[l, 1, :, NBAND + at : NBAND + at + 128] = -re
        return carry

    lax.fori_loop(0, blocks, block_step, 0)

    def send(o):
        d = lax.rem(c + o, peers)
        return pltpu.make_async_remote_copy(
            src_ref=outbox.at[o - 1],
            dst_ref=inbox.at[o - 1],
            send_sem=ch_send.at[o - 1],
            recv_sem=ch_recv.at[o - 1],
            device_id={"chan": d},
        )

    for o in range(1, peers):
        d = lax.rem(c + o, peers)
        outbox[o - 1] = paired[send_ref[0, 0, d, 0], 0]
        send(o).start()

    out_ref[0, 0, c] = jnp.zeros(out_ref.shape[3:], out_ref.dtype)
    flat = paired.shape[0] * paired.shape[1] * BLOCK
    for o in range(1, peers):
        p = lax.rem(c - o + peers, peers)
        send(o).wait_recv()
        left = paired[...].reshape(flat, 2 * NBAND)
        value = lax.dot_general(
            left, inbox[o - 1], (((1,), (1,)), ((), ())), preferred_element_type=jnp.float32
        )
        value = value * (1.0 / math.sqrt(NBAND))
        value = jnp.where(count_ref[0, 0, p] > 0, value, 0.0)
        out_ref[0, 0, p] = value.astype(out_ref.dtype).reshape(out_ref.shape[3:])

    for l in range(blocks):
        for o in range(1, teams):
            part(o, l).wait_send()
    for o in range(1, peers):
        send(o).wait_send()


def local(peers, teams, raw, send_blocks, pair_count):
    table = jnp.asarray(dft_table(), dtype=jnp.bfloat16)
    bands = jnp.asarray(filter_bands())
    ones = jnp.asarray(segment_ones())
    blocks = raw.shape[0] // (teams * BLOCK)
    vmem = pl.BlockSpec(memory_space=pltpu.VMEM)
    smem = pl.BlockSpec(memory_space=pltpu.SMEM)
    anywhere = pl.BlockSpec(memory_space=pl.ANY)
    return pl.pallas_call(
        functools.partial(kernel, peers, teams),
        out_shape=jax.ShapeDtypeStruct((1, 1, peers, 1, blocks, 2, BLOCK, BLOCK), jnp.bfloat16),
        in_specs=[anywhere, anywhere, vmem, vmem, smem, smem],
        out_specs=vmem,
        scratch_shapes=[
            pltpu.VMEM((blocks, BLOCK, NT), jnp.bfloat16),
            pltpu.VMEM((NT, 2 * NBAND), jnp.bfloat16),
            pltpu.VMEM((BLOCK, NT), jnp.bfloat16),
            pltpu.VMEM((blocks, 2, BLOCK, 2 * NBAND), jnp.bfloat16),
            pltpu.VMEM((peers - 1, BLOCK, 2 * NBAND), jnp.bfloat16),
            pltpu.VMEM((peers - 1, BLOCK, 2 * NBAND), jnp.bfloat16),
            pltpu.SemaphoreType.DMA,
            pltpu.SemaphoreType.DMA((blocks,)),
            pltpu.SemaphoreType.DMA((teams - 1, blocks)),
            pltpu.SemaphoreType.DMA((teams - 1, blocks)),
            pltpu.SemaphoreType.DMA((peers - 1,)),
            pltpu.SemaphoreType.DMA((peers - 1,)),
        ],
        compiler_params=pltpu.CompilerParams(
            collective_id=0, has_side_effects=True, vmem_limit_bytes=48 * 1024 * 1024
        ),
        cost_estimate=pl.CostEstimate(
            flops=3_000_000_000, bytes_accessed=6_000_000, transcendentals=0
        ),
    )(raw, table, bands, ones, send_blocks, pair_count)


def solution(mesh):
    return jax.shard_map(
        functools.partial(local, mesh.shape["chan"], mesh.shape["tm"]),
        mesh=mesh,
        in_specs=(P(("groups", "chan"), "tm"), P("chan", "tm", None, None), P("chan", "tm", None)),
        out_specs=P(("groups", "chan"), "tm", None, None, None, None, None, None),
        check_vma=False,
    )
```

```python
import functools
import math

import jax
import jax.numpy as jnp
import numpy as np
from jax import lax
from jax.experimental import pallas as pl
from jax.experimental.pallas import tpu as pltpu
from jax.sharding import PartitionSpec as P

BLOCK = 128
NT = 2048
F0 = 128
NBAND = 512
SUBW = 64
RAD = 15
TILE = 256
CHUNK = 128
CHUNKS = NBAND // CHUNK
SIDE = 128


def sinc_value(arg):
    if arg == 0:
        return 1.0
    return math.sin(math.pi * arg) / (math.pi * arg)


def filter_taps():
    low = F0 / NT
    high = (F0 + NBAND) / NT
    taps = []
    for offset in range(-RAD, RAD + 1):
        value = 2.0 * high * sinc_value(2.0 * high * offset) - 2.0 * low * sinc_value(
            2.0 * low * offset
        )
        value = value * (0.5 + 0.5 * math.cos(math.pi * offset / (RAD + 1)))
        taps.append(value)
    return taps


def dft_table():
    samples = np.arange(NT)[:, None]
    freqs = np.arange(F0, F0 + NBAND)[None, :]
    phase = samples * freqs % NT
    angle = 2.0 * np.pi * phase / NT
    return np.concatenate([np.cos(angle), -np.sin(angle)], axis=1)


def filter_bands():
    taps = np.asarray(filter_taps(), np.float64).astype(np.float32)
    u = np.arange(TILE + 2 * SIDE)[:, None]
    v = np.arange(TILE)[None, :]
    k = v + SIDE - u
    band = np.where(np.abs(k) <= RAD, taps[np.clip(k + RAD, 0, 2 * RAD)], 0).astype(np.float32)
    first = band.astype(jnp.bfloat16)
    second = (band - first.astype(np.float32)).astype(jnp.bfloat16)
    return np.stack([first, second])


def segment_ones():
    run = np.arange(128) // SUBW
    return (run[:, None] == run[None, :]).astype(jnp.bfloat16)


def dot(a, b):
    return jnp.dot(a, b, preferred_element_type=jnp.float32)


def kernel(
    peers,
    teams,
    raw_ref,
    table_ref,
    bands_ref,
    ones_ref,
    send_ref,
    count_ref,
    out_ref,
    rows,
    table,
    bands,
    ones,
    filtered,
    paired,
    outbox,
    inbox,
    load_sem,
    own_sem,
    tm_send,
    tm_recv,
    ch_send,
    ch_recv,
):
    c = lax.axis_index("chan")
    t = lax.axis_index("tm")
    blocks = rows.shape[0]
    span = raw_ref.shape[1]

    loads = [
        pltpu.make_async_copy(bands_ref, bands, load_sem.at[0]),
        pltpu.make_async_copy(ones_ref, ones, load_sem.at[1]),
        pltpu.make_async_copy(table_ref, table, load_sem.at[2]),
    ]
    for load in loads:
        load.start()

    barrier = pltpu.get_barrier_semaphore()
    for o in range(1, teams):
        pl.semaphore_signal(barrier, inc=1, device_id={"tm": lax.rem(t + o, teams)})
    for o in range(1, peers):
        pl.semaphore_signal(barrier, inc=1, device_id={"chan": lax.rem(c + o, peers)})
    pl.semaphore_wait(barrier, teams + peers - 2)

    mine = pl.ds(pl.multiple_of(t * span, 128), span)

    def part(o, l):
        q = lax.rem(t + o, teams)
        start = pl.multiple_of((q * blocks + l) * BLOCK, BLOCK)
        return pltpu.make_async_remote_copy(
            src_ref=raw_ref.at[pl.ds(start, BLOCK), :],
            dst_ref=rows.at[l, :, mine],
            send_sem=tm_send.at[o - 1, l],
            recv_sem=tm_recv.at[o - 1, l],
            device_id={"tm": q},
        )

    def own(l):
        start = pl.multiple_of((t * blocks + l) * BLOCK, BLOCK)
        return pltpu.make_async_copy(
            raw_ref.at[pl.ds(start, BLOCK), :], rows.at[l, :, mine], own_sem.at[l]
        )

    for l in range(blocks):
        for o in range(1, teams):
            part(o, l).start()
        own(l).start()
    out_ref[0, 0, c] = jnp.zeros(out_ref.shape[3:], out_ref.dtype)
    for load in loads:
        load.wait()

    def filter_block(l, carry):
        own(l).wait()
        for o in range(1, teams):
            part(o, l).wait_recv()
        for j in range(NT // TILE):
            lo, hi = j * TILE - SIDE, (j + 1) * TILE + SIDE
            if lo < 0:
                window = jnp.concatenate([rows[l, :, NT + lo :], rows[l, :, :hi]], axis=1)
            elif hi > NT:
                window = jnp.concatenate([rows[l, :, lo:], rows[l, :, : hi - NT]], axis=1)
            else:
                window = rows[l, :, lo:hi]
            value = dot(window, bands[0]) + dot(window, bands[1])
            filtered[l, :, j * TILE : (j + 1) * TILE] = value.astype(jnp.bfloat16)
        return carry

    lax.fori_loop(0, blocks, filter_block, 0)

    def send(o, k):
        return pltpu.make_async_remote_copy(
            src_ref=outbox.at[o - 1, k],
            dst_ref=inbox.at[o - 1, k],
            send_sem=ch_send.at[o - 1, k],
            recv_sem=ch_recv.at[o - 1, k],
            device_id={"chan": lax.rem(c + o, peers)},
        )

    for k in range(CHUNKS):
        at = k * 2 * CHUNK
        signal = filtered[...].reshape(blocks * BLOCK, NT)
        value = dot(signal, table[:, at : at + 2 * CHUNK])
        real, imag = value[:, :CHUNK], value[:, CHUNK:]
        power = real * real + imag * imag
        first = power.astype(jnp.bfloat16)
        second = (power - first.astype(jnp.float32)).astype(jnp.bfloat16)
        total = dot(first, ones[...]) + dot(second, ones[...])
        level = lax.rsqrt(total * (1.0 / SUBW) + 1e-06)
        re = (real * level).astype(jnp.bfloat16).reshape(blocks, BLOCK, CHUNK)
        im = (imag * level).astype(jnp.bfloat16).reshape(blocks, BLOCK, CHUNK)
        paired[k, :, 0, :, :CHUNK] = re
        paired[k, :, 0, :, CHUNK:] = im
        for o in range(1, peers):
            outbox[o - 1, k] = paired[k, send_ref[lax.rem(c + o, peers)], 0]
            send(o, k).start()
        paired[k, :, 1, :, :CHUNK] = im
        paired[k, :, 1, :, CHUNK:] = -re

    flat = 2 * blocks * BLOCK
    for o in range(1, peers):
        p = lax.rem(c - o + peers, peers)
        value = jnp.zeros((flat, BLOCK), jnp.float32)
        for k in range(CHUNKS):
            send(o, k).wait_recv()
            value = value + lax.dot_general(
                paired[k].reshape(flat, 2 * CHUNK),
                inbox[o - 1, k],
                (((1,), (1,)), ((), ())),
                preferred_element_type=jnp.float32,
            )
        value = value * (1.0 / math.sqrt(NBAND))
        value = jnp.where(count_ref[p] > 0, value, 0.0)
        out_ref[0, 0, p] = value.astype(out_ref.dtype).reshape(out_ref.shape[3:])

    for l in range(blocks):
        for o in range(1, teams):
            part(o, l).wait_send()
    for o in range(1, peers):
        for k in range(CHUNKS):
            send(o, k).wait_send()


def local(peers, teams, raw, send_blocks, pair_count):
    table = dft_table().reshape(NT, 2, CHUNKS, CHUNK).transpose(0, 2, 1, 3)
    table = jnp.asarray(table.reshape(NT, 2 * NBAND), dtype=jnp.bfloat16)
    bands = jnp.asarray(filter_bands())
    ones = jnp.asarray(segment_ones())
    blocks = raw.shape[0] // (teams * BLOCK)
    vmem = pl.BlockSpec(memory_space=pltpu.VMEM)
    smem = pl.BlockSpec(memory_space=pltpu.SMEM)
    anywhere = pl.BlockSpec(memory_space=pl.ANY)
    return pl.pallas_call(
        functools.partial(kernel, peers, teams),
        out_shape=jax.ShapeDtypeStruct((1, 1, peers, 1, blocks, 2, BLOCK, BLOCK), jnp.bfloat16),
        in_specs=[anywhere, anywhere, anywhere, anywhere, smem, smem],
        out_specs=vmem,
        scratch_shapes=[
            pltpu.VMEM((blocks, BLOCK, NT), jnp.bfloat16),
            pltpu.VMEM(table.shape, jnp.bfloat16),
            pltpu.VMEM(bands.shape, jnp.bfloat16),
            pltpu.VMEM(ones.shape, jnp.bfloat16),
            pltpu.VMEM((blocks, BLOCK, NT), jnp.bfloat16),
            pltpu.VMEM((CHUNKS, blocks, 2, BLOCK, 2 * CHUNK), jnp.bfloat16),
            pltpu.VMEM((peers - 1, CHUNKS, BLOCK, 2 * CHUNK), jnp.bfloat16),
            pltpu.VMEM((peers - 1, CHUNKS, BLOCK, 2 * CHUNK), jnp.bfloat16),
            pltpu.SemaphoreType.DMA((3,)),
            pltpu.SemaphoreType.DMA((blocks,)),
            pltpu.SemaphoreType.DMA((teams - 1, blocks)),
            pltpu.SemaphoreType.DMA((teams - 1, blocks)),
            pltpu.SemaphoreType.DMA((peers - 1, CHUNKS)),
            pltpu.SemaphoreType.DMA((peers - 1, CHUNKS)),
        ],
        compiler_params=pltpu.CompilerParams(
            collective_id=0, has_side_effects=True, vmem_limit_bytes=62 * 1024 * 1024
        ),
        cost_estimate=pl.CostEstimate(
            flops=3_000_000_000, bytes_accessed=6_000_000, transcendentals=0
        ),
    )(raw, table, bands, ones, send_blocks.reshape(peers), pair_count.reshape(peers))


def solution(mesh):
    return jax.shard_map(
        functools.partial(local, mesh.shape["chan"], mesh.shape["tm"]),
        mesh=mesh,
        in_specs=(P(("groups", "chan"), "tm"), P("chan", "tm", None, None), P("chan", "tm", None)),
        out_specs=P(("groups", "chan"), "tm", None, None, None, None, None, None),
        check_vma=False,
    )
```

```python
import functools
import math

import jax
import jax.numpy as jnp
import numpy as np
from jax import lax
from jax.experimental import pallas as pl
from jax.experimental.pallas import tpu as pltpu
from jax.sharding import PartitionSpec as P

BLOCK = 128
NT = 2048
F0 = 128
NBAND = 512
SUBW = 64
RAD = 15
TILE = 256
CHUNK = 128
CHUNKS = NBAND // CHUNK
SIDE = 128


def sinc_value(arg):
    if arg == 0:
        return 1.0
    return math.sin(math.pi * arg) / (math.pi * arg)


def filter_taps():
    low = F0 / NT
    high = (F0 + NBAND) / NT
    taps = []
    for offset in range(-RAD, RAD + 1):
        value = 2.0 * high * sinc_value(2.0 * high * offset) - 2.0 * low * sinc_value(
            2.0 * low * offset
        )
        value = value * (0.5 + 0.5 * math.cos(math.pi * offset / (RAD + 1)))
        taps.append(value)
    return taps


def dft_table():
    samples = np.arange(NT)[:, None]
    freqs = np.arange(F0, F0 + NBAND)[None, :]
    phase = samples * freqs % NT
    angle = 2.0 * np.pi * phase / NT
    return np.concatenate([np.cos(angle), -np.sin(angle)], axis=1)


def filter_bands():
    taps = np.asarray(filter_taps(), np.float64).astype(np.float32)
    u = np.arange(TILE + 2 * SIDE)[:, None]
    v = np.arange(TILE)[None, :]
    k = v + SIDE - u
    band = np.where(np.abs(k) <= RAD, taps[np.clip(k + RAD, 0, 2 * RAD)], 0).astype(np.float32)
    first = band.astype(jnp.bfloat16)
    second = (band - first.astype(np.float32)).astype(jnp.bfloat16)
    return np.stack([first, second])


def segment_ones():
    run = np.arange(128) // SUBW
    return (run[:, None] == run[None, :]).astype(jnp.bfloat16)


def dot(a, b):
    return jnp.dot(a, b, preferred_element_type=jnp.float32)


def kernel(
    peers,
    teams,
    raw_ref,
    table_ref,
    bands_ref,
    ones_ref,
    send_ref,
    count_ref,
    out_ref,
    rows,
    table,
    bands,
    ones,
    filtered,
    paired,
    outbox,
    inbox,
    load_sem,
    own_sem,
    tm_send,
    tm_recv,
    ch_send,
    ch_recv,
    choices,
    chosen,
    crossed,
    handed,
    choice_sem,
    cross_send,
    cross_recv,
    hand_send,
):
    c = lax.axis_index("chan")
    t = lax.axis_index("tm")
    blocks = rows.shape[0]
    span = raw_ref.shape[1]

    relay = peers == 4 and blocks == 2
    inner = jnp.logical_and(relay, jnp.logical_and(c > 0, c < 3))
    partner = 3 - c

    def direct(o):
        return jnp.logical_or(jnp.logical_not(inner), o == 5 - 2 * c)

    def arrives(o):
        return jnp.logical_or(jnp.logical_not(inner), o != 5 - 2 * c)

    def put(slot, k, value):
        inbox[slot, k] = value

    def choice():
        return pltpu.make_async_remote_copy(
            src_ref=choices,
            dst_ref=chosen,
            send_sem=choice_sem.at[0],
            recv_sem=choice_sem.at[1],
            device_id={"chan": partner},
        )

    loads = [
        pltpu.make_async_copy(bands_ref, bands, load_sem.at[0]),
        pltpu.make_async_copy(ones_ref, ones, load_sem.at[1]),
        pltpu.make_async_copy(table_ref, table, load_sem.at[2]),
    ]
    for load in loads:
        load.start()

    barrier = pltpu.get_barrier_semaphore()
    for o in range(1, teams):
        pl.semaphore_signal(barrier, inc=1, device_id={"tm": lax.rem(t + o, teams)})
    for o in range(1, peers):
        pl.semaphore_signal(barrier, inc=1, device_id={"chan": lax.rem(c + o, peers)})
    pl.semaphore_wait(barrier, teams + peers - 2)

    mine = pl.ds(pl.multiple_of(t * span, 128), span)

    def part(o, l):
        q = lax.rem(t + o, teams)
        start = pl.multiple_of((q * blocks + l) * BLOCK, BLOCK)
        return pltpu.make_async_remote_copy(
            src_ref=raw_ref.at[pl.ds(start, BLOCK), :],
            dst_ref=rows.at[l, :, mine],
            send_sem=tm_send.at[o - 1, l],
            recv_sem=tm_recv.at[o - 1, l],
            device_id={"tm": q},
        )

    def own(l):
        start = pl.multiple_of((t * blocks + l) * BLOCK, BLOCK)
        return pltpu.make_async_copy(
            raw_ref.at[pl.ds(start, BLOCK), :], rows.at[l, :, mine], own_sem.at[l]
        )

    for l in range(blocks):
        for o in range(1, teams):
            part(o, l).start()
        own(l).start()
    if relay:

        @pl.when(inner)
        def _():
            choices[0] = jnp.full((8, 128), send_ref[partner], jnp.int32)
            choices[1] = jnp.full((8, 128), send_ref[6 - 3 * c], jnp.int32)
            choice().start()

    out_ref[0, 0, c] = jnp.zeros(out_ref.shape[3:], out_ref.dtype)
    for load in loads:
        load.wait()

    def filter_block(l):
        own(l).wait()
        for o in range(1, teams):
            part(o, l).wait_recv()
        for j in range(NT // TILE):
            lo, hi = j * TILE - SIDE, (j + 1) * TILE + SIDE
            if lo < 0:
                window = jnp.concatenate([rows[l, :, NT + lo :], rows[l, :, :hi]], axis=1)
            elif hi > NT:
                window = jnp.concatenate([rows[l, :, lo:], rows[l, :, : hi - NT]], axis=1)
            else:
                window = rows[l, :, lo:hi]
            value = dot(window, bands[0]) + dot(window, bands[1])
            filtered[l, :, j * TILE : (j + 1) * TILE] = value.astype(jnp.bfloat16)

    def whiten_chunk(l, k):
        at = k * 2 * CHUNK
        value = dot(filtered[l], table[:, at : at + 2 * CHUNK])
        real, imag = value[:, :CHUNK], value[:, CHUNK:]
        power = real * real + imag * imag
        first = power.astype(jnp.bfloat16)
        second = (power - first.astype(jnp.float32)).astype(jnp.bfloat16)
        total = dot(first, ones[...]) + dot(second, ones[...])
        level = lax.rsqrt(total * (1.0 / SUBW) + 1e-06)
        re = (real * level).astype(jnp.bfloat16)
        im = (imag * level).astype(jnp.bfloat16)
        paired[k, l, 0, :, :CHUNK] = re
        paired[k, l, 0, :, CHUNK:] = im
        paired[k, l, 1, :, :CHUNK] = im
        paired[k, l, 1, :, CHUNK:] = -re

    def send(o, k):
        return pltpu.make_async_remote_copy(
            src_ref=outbox.at[o - 1, k],
            dst_ref=inbox.at[o - 1, k],
            send_sem=ch_send.at[o - 1, k],
            recv_sem=ch_recv.at[o - 1, k],
            device_id={"chan": lax.rem(c + o, peers)},
        )

    def cross(l, k):
        return pltpu.make_async_remote_copy(
            src_ref=paired.at[k, l, 0],
            dst_ref=crossed.at[l, k],
            send_sem=cross_send.at[l, k],
            recv_sem=cross_recv.at[l, k],
            device_id={"chan": partner},
        )

    def hand_on(k):
        return pltpu.make_async_remote_copy(
            src_ref=handed.at[k],
            dst_ref=inbox.at[1, k],
            send_sem=hand_send.at[k],
            recv_sem=ch_recv.at[1, k],
            device_id={"chan": 3 * (c - 1)},
        )

    def start_send(o, k):
        outbox[o - 1, k] = paired[k, send_ref[lax.rem(c + o, peers)], 0]
        send(o, k).start()

    for l in range(blocks):
        filter_block(l)
        for k in range(CHUNKS):
            whiten_chunk(l, k)
            if relay:
                pl.when(inner)(lambda l=l, k=k: cross(l, k).start())
            if l == blocks - 1:
                for o in range(1, peers):
                    pl.when(direct(o))(lambda o=o, k=k: start_send(o, k))

    if relay:

        @pl.when(inner)
        def _():
            choice().wait_recv()
            for_me = jnp.concatenate([chosen[0, :1], chosen[0, :1]], axis=1) > 0
            for_next = jnp.concatenate([chosen[1, :1], chosen[1, :1]], axis=1) > 0
            for k in range(CHUNKS):
                for l in range(blocks):
                    cross(l, k).wait_recv()
                zero = crossed[0, k].astype(jnp.float32)
                one = crossed[1, k].astype(jnp.float32)
                handed[k] = jnp.where(for_next, one, zero).astype(jnp.bfloat16)
                hand_on(k).start()
                mine_now = jnp.where(for_me, one, zero).astype(jnp.bfloat16)
                pl.when(c == 1)(lambda k=k, v=mine_now: put(2, k, v))
                pl.when(c == 2)(lambda k=k, v=mine_now: put(0, k, v))

    flat = 2 * blocks * BLOCK
    for o in range(1, peers):
        p = lax.rem(c - o + peers, peers)
        value = jnp.zeros((flat, BLOCK), jnp.float32)
        for k in range(CHUNKS):
            pl.when(arrives(o))(lambda o=o, k=k: send(o, k).wait_recv())
            value = value + lax.dot_general(
                paired[k].reshape(flat, 2 * CHUNK),
                inbox[o - 1, k],
                (((1,), (1,)), ((), ())),
                preferred_element_type=jnp.float32,
            )
        value = value * (1.0 / math.sqrt(NBAND))
        value = jnp.where(count_ref[p] > 0, value, 0.0)
        out_ref[0, 0, p] = value.astype(out_ref.dtype).reshape(out_ref.shape[3:])

    for l in range(blocks):
        for o in range(1, teams):
            part(o, l).wait_send()
    for o in range(1, peers):
        for k in range(CHUNKS):
            pl.when(direct(o))(lambda o=o, k=k: send(o, k).wait_send())
    if relay:

        @pl.when(inner)
        def _():
            choice().wait_send()
            for k in range(CHUNKS):
                hand_on(k).wait_send()
                for l in range(blocks):
                    cross(l, k).wait_send()


def local(peers, teams, raw, send_blocks, pair_count):
    table = dft_table().reshape(NT, 2, CHUNKS, CHUNK).transpose(0, 2, 1, 3)
    table = jnp.asarray(table.reshape(NT, 2 * NBAND), dtype=jnp.bfloat16)
    bands = jnp.asarray(filter_bands())
    ones = jnp.asarray(segment_ones())
    blocks = raw.shape[0] // (teams * BLOCK)
    vmem = pl.BlockSpec(memory_space=pltpu.VMEM)
    smem = pl.BlockSpec(memory_space=pltpu.SMEM)
    anywhere = pl.BlockSpec(memory_space=pl.ANY)
    return pl.pallas_call(
        functools.partial(kernel, peers, teams),
        out_shape=jax.ShapeDtypeStruct((1, 1, peers, 1, blocks, 2, BLOCK, BLOCK), jnp.bfloat16),
        in_specs=[anywhere, anywhere, anywhere, anywhere, smem, smem],
        out_specs=vmem,
        scratch_shapes=[
            pltpu.VMEM((blocks, BLOCK, NT), jnp.bfloat16),
            pltpu.VMEM(table.shape, jnp.bfloat16),
            pltpu.VMEM(bands.shape, jnp.bfloat16),
            pltpu.VMEM(ones.shape, jnp.bfloat16),
            pltpu.VMEM((blocks, BLOCK, NT), jnp.bfloat16),
            pltpu.VMEM((CHUNKS, blocks, 2, BLOCK, 2 * CHUNK), jnp.bfloat16),
            pltpu.VMEM((peers - 1, CHUNKS, BLOCK, 2 * CHUNK), jnp.bfloat16),
            pltpu.VMEM((peers - 1, CHUNKS, BLOCK, 2 * CHUNK), jnp.bfloat16),
            pltpu.SemaphoreType.DMA((3,)),
            pltpu.SemaphoreType.DMA((blocks,)),
            pltpu.SemaphoreType.DMA((teams - 1, blocks)),
            pltpu.SemaphoreType.DMA((teams - 1, blocks)),
            pltpu.SemaphoreType.DMA((peers - 1, CHUNKS)),
            pltpu.SemaphoreType.DMA((peers - 1, CHUNKS)),
            pltpu.VMEM((2, 8, 128), jnp.int32),
            pltpu.VMEM((2, 8, 128), jnp.int32),
            pltpu.VMEM((blocks, CHUNKS, BLOCK, 2 * CHUNK), jnp.bfloat16),
            pltpu.VMEM((CHUNKS, BLOCK, 2 * CHUNK), jnp.bfloat16),
            pltpu.SemaphoreType.DMA((2,)),
            pltpu.SemaphoreType.DMA((blocks, CHUNKS)),
            pltpu.SemaphoreType.DMA((blocks, CHUNKS)),
            pltpu.SemaphoreType.DMA((CHUNKS,)),
        ],
        compiler_params=pltpu.CompilerParams(
            collective_id=0, has_side_effects=True, vmem_limit_bytes=62 * 1024 * 1024
        ),
        cost_estimate=pl.CostEstimate(
            flops=3_000_000_000, bytes_accessed=6_000_000, transcendentals=0
        ),
    )(raw, table, bands, ones, send_blocks.reshape(peers), pair_count.reshape(peers))


def solution(mesh):
    return jax.shard_map(
        functools.partial(local, mesh.shape["chan"], mesh.shape["tm"]),
        mesh=mesh,
        in_specs=(P(("groups", "chan"), "tm"), P("chan", "tm", None, None), P("chan", "tm", None)),
        out_specs=P(("groups", "chan"), "tm", None, None, None, None, None, None),
        check_vma=False,
    )
```

```python
import functools
import math

import jax
import jax.numpy as jnp
import numpy as np
from jax import lax
from jax.experimental import pallas as pl
from jax.experimental.pallas import tpu as pltpu
from jax.sharding import PartitionSpec as P

BLOCK = 128
NT = 2048
F0 = 128
NBAND = 512
SUBW = 64
RAD = 15
TILE = 256
CHUNK = 128
CHUNKS = NBAND // CHUNK
SIDE = 128


def sinc_value(arg):
    if arg == 0:
        return 1.0
    return math.sin(math.pi * arg) / (math.pi * arg)


def filter_taps():
    low = F0 / NT
    high = (F0 + NBAND) / NT
    taps = []
    for offset in range(-RAD, RAD + 1):
        value = 2.0 * high * sinc_value(2.0 * high * offset) - 2.0 * low * sinc_value(
            2.0 * low * offset
        )
        value = value * (0.5 + 0.5 * math.cos(math.pi * offset / (RAD + 1)))
        taps.append(value)
    return taps


def dft_table():
    samples = np.arange(NT)[:, None]
    freqs = np.arange(F0, F0 + NBAND)[None, :]
    phase = samples * freqs % NT
    angle = 2.0 * np.pi * phase / NT
    return np.concatenate([np.cos(angle), -np.sin(angle)], axis=1)


def filter_bands():
    taps = np.asarray(filter_taps(), np.float64).astype(np.float32)
    u = np.arange(TILE + 2 * SIDE)[:, None]
    v = np.arange(TILE)[None, :]
    k = v + SIDE - u
    band = np.where(np.abs(k) <= RAD, taps[np.clip(k + RAD, 0, 2 * RAD)], 0).astype(np.float32)
    first = band.astype(jnp.bfloat16)
    second = (band - first.astype(np.float32)).astype(jnp.bfloat16)
    return np.stack([first, second])


def segment_ones():
    run = np.arange(128) // SUBW
    return (run[:, None] == run[None, :]).astype(jnp.bfloat16)


def dot(a, b):
    return jnp.dot(a, b, preferred_element_type=jnp.float32)


def kernel(
    peers,
    teams,
    raw_ref,
    table_ref,
    bands_ref,
    ones_ref,
    send_ref,
    out_ref,
    rows,
    table,
    bands,
    ones,
    filtered,
    paired,
    outbox,
    inbox,
    load_sem,
    own_sem,
    tm_send,
    tm_recv,
    ch_send,
    ch_recv,
    choices,
    chosen,
    crossed,
    handed,
    choice_sem,
    cross_send,
    cross_recv,
    hand_send,
):
    c = lax.axis_index("chan")
    t = lax.axis_index("tm")
    blocks = rows.shape[0]
    span = raw_ref.shape[1]

    relay = peers == 4 and blocks == 2
    inner = jnp.logical_and(relay, jnp.logical_and(c > 0, c < 3))
    partner = 3 - c

    def direct(o):
        return jnp.logical_or(jnp.logical_not(inner), o == 5 - 2 * c)

    def arrives(o):
        return jnp.logical_or(jnp.logical_not(inner), o != 5 - 2 * c)

    def put(slot, k, value):
        inbox[slot, k] = value

    def choice():
        return pltpu.make_async_remote_copy(
            src_ref=choices,
            dst_ref=chosen,
            send_sem=choice_sem.at[0],
            recv_sem=choice_sem.at[1],
            device_id={"chan": partner},
        )

    loads = [
        pltpu.make_async_copy(bands_ref, bands, load_sem.at[0]),
        pltpu.make_async_copy(ones_ref, ones, load_sem.at[1]),
        pltpu.make_async_copy(table_ref, table, load_sem.at[2]),
    ]
    for load in loads:
        load.start()

    barrier = pltpu.get_barrier_semaphore()
    for o in range(1, teams):
        pl.semaphore_signal(barrier, inc=1, device_id={"tm": lax.rem(t + o, teams)})
    for o in range(1, peers):
        pl.semaphore_signal(barrier, inc=1, device_id={"chan": lax.rem(c + o, peers)})
    pl.semaphore_wait(barrier, teams + peers - 2)

    mine = pl.ds(pl.multiple_of(t * span, 128), span)

    def part(o, l):
        q = lax.rem(t + o, teams)
        start = pl.multiple_of((q * blocks + l) * BLOCK, BLOCK)
        return pltpu.make_async_remote_copy(
            src_ref=raw_ref.at[pl.ds(start, BLOCK), :],
            dst_ref=rows.at[l, :, mine],
            send_sem=tm_send.at[o - 1, l],
            recv_sem=tm_recv.at[o - 1, l],
            device_id={"tm": q},
        )

    def own(l):
        start = pl.multiple_of((t * blocks + l) * BLOCK, BLOCK)
        return pltpu.make_async_copy(
            raw_ref.at[pl.ds(start, BLOCK), :], rows.at[l, :, mine], own_sem.at[l]
        )

    for l in range(blocks):
        for o in range(1, teams):
            part(o, l).start()
        own(l).start()
    if relay:

        @pl.when(inner)
        def _():
            choices[0] = jnp.full((8, 128), send_ref[partner], jnp.int32)
            choices[1] = jnp.full((8, 128), send_ref[6 - 3 * c], jnp.int32)
            choice().start()

    out_ref[0, 0, c] = jnp.zeros(out_ref.shape[3:], out_ref.dtype)
    for load in loads:
        load.wait()

    def filter_block(l):
        own(l).wait()
        for o in range(1, teams):
            part(o, l).wait_recv()
        for j in range(NT // TILE):
            lo, hi = j * TILE - SIDE, (j + 1) * TILE + SIDE
            if lo < 0:
                window = jnp.concatenate([rows[l, :, NT + lo :], rows[l, :, :hi]], axis=1)
            elif hi > NT:
                window = jnp.concatenate([rows[l, :, lo:], rows[l, :, : hi - NT]], axis=1)
            else:
                window = rows[l, :, lo:hi]
            value = dot(window, bands[0]) + dot(window, bands[1])
            filtered[l, :, j * TILE : (j + 1) * TILE] = value.astype(jnp.bfloat16)

    def whiten_chunk(l, k):
        at = k * 2 * CHUNK
        value = dot(filtered[l], table[:, at : at + 2 * CHUNK])
        real, imag = value[:, :CHUNK], value[:, CHUNK:]
        power = real * real + imag * imag
        first = power.astype(jnp.bfloat16)
        second = (power - first.astype(jnp.float32)).astype(jnp.bfloat16)
        total = dot(first, ones[...]) + dot(second, ones[...])
        level = lax.rsqrt(total * (1.0 / SUBW) + 1e-06)
        re = (real * level).astype(jnp.bfloat16)
        im = (imag * level).astype(jnp.bfloat16)
        paired[k, l, 0, :, :CHUNK] = re
        paired[k, l, 0, :, CHUNK:] = im
        paired[k, l, 1, :, :CHUNK] = im
        paired[k, l, 1, :, CHUNK:] = -re

    def send(o, k):
        return pltpu.make_async_remote_copy(
            src_ref=outbox.at[o - 1, k],
            dst_ref=inbox.at[o - 1, k],
            send_sem=ch_send.at[o - 1, k],
            recv_sem=ch_recv.at[o - 1, k],
            device_id={"chan": lax.rem(c + o, peers)},
        )

    def cross(l, k):
        return pltpu.make_async_remote_copy(
            src_ref=paired.at[k, l, 0],
            dst_ref=crossed.at[l, k],
            send_sem=cross_send.at[l, k],
            recv_sem=cross_recv.at[l, k],
            device_id={"chan": partner},
        )

    def hand_on(k):
        return pltpu.make_async_remote_copy(
            src_ref=handed.at[k],
            dst_ref=inbox.at[1, k],
            send_sem=hand_send.at[k],
            recv_sem=ch_recv.at[1, k],
            device_id={"chan": 3 * (c - 1)},
        )

    def start_send(o, k):
        outbox[o - 1, k] = paired[k, send_ref[lax.rem(c + o, peers)], 0]
        send(o, k).start()

    for l in range(blocks):
        filter_block(l)
        for k in range(CHUNKS):
            whiten_chunk(l, k)
            if relay:
                pl.when(inner)(lambda l=l, k=k: cross(l, k).start())
            if l == blocks - 1:
                for o in range(1, peers):
                    pl.when(direct(o))(lambda o=o, k=k: start_send(o, k))

    if relay:

        @pl.when(inner)
        def _():
            choice().wait_recv()
            for_me = jnp.concatenate([chosen[0, :1], chosen[0, :1]], axis=1) > 0
            for_next = jnp.concatenate([chosen[1, :1], chosen[1, :1]], axis=1) > 0
            for k in range(CHUNKS):
                for l in range(blocks):
                    cross(l, k).wait_recv()
                zero = crossed[0, k].astype(jnp.float32)
                one = crossed[1, k].astype(jnp.float32)
                handed[k] = jnp.where(for_next, one, zero).astype(jnp.bfloat16)
                hand_on(k).start()
                mine_now = jnp.where(for_me, one, zero).astype(jnp.bfloat16)
                pl.when(c == 1)(lambda k=k, v=mine_now: put(2, k, v))
                pl.when(c == 2)(lambda k=k, v=mine_now: put(0, k, v))

    flat = 2 * blocks * BLOCK
    for o in range(1, peers):
        p = lax.rem(c - o + peers, peers)
        value = jnp.zeros((flat, BLOCK), jnp.float32)
        for k in range(CHUNKS):
            pl.when(arrives(o))(lambda o=o, k=k: send(o, k).wait_recv())
            value = value + lax.dot_general(
                paired[k].reshape(flat, 2 * CHUNK),
                inbox[o - 1, k],
                (((1,), (1,)), ((), ())),
                preferred_element_type=jnp.float32,
            )
        value = value * (1.0 / math.sqrt(NBAND))
        out_ref[0, 0, p] = value.astype(out_ref.dtype).reshape(out_ref.shape[3:])

    for l in range(blocks):
        for o in range(1, teams):
            part(o, l).wait_send()
    for o in range(1, peers):
        for k in range(CHUNKS):
            pl.when(direct(o))(lambda o=o, k=k: send(o, k).wait_send())
    if relay:

        @pl.when(inner)
        def _():
            choice().wait_send()
            for k in range(CHUNKS):
                hand_on(k).wait_send()
                for l in range(blocks):
                    cross(l, k).wait_send()


def local(peers, teams, raw, send_blocks, pair_count):
    table = dft_table().reshape(NT, 2, CHUNKS, CHUNK).transpose(0, 2, 1, 3)
    table = jnp.asarray(table.reshape(NT, 2 * NBAND), dtype=jnp.bfloat16)
    bands = jnp.asarray(filter_bands())
    ones = jnp.asarray(segment_ones())
    blocks = raw.shape[0] // (teams * BLOCK)
    vmem = pl.BlockSpec(memory_space=pltpu.VMEM)
    smem = pl.BlockSpec(memory_space=pltpu.SMEM)
    anywhere = pl.BlockSpec(memory_space=pl.ANY)
    result = pl.pallas_call(
        functools.partial(kernel, peers, teams),
        out_shape=jax.ShapeDtypeStruct((1, 1, peers, 1, blocks, 2, BLOCK, BLOCK), jnp.bfloat16),
        in_specs=[anywhere, anywhere, anywhere, anywhere, smem],
        out_specs=vmem,
        scratch_shapes=[
            pltpu.VMEM((blocks, BLOCK, NT), jnp.bfloat16),
            pltpu.VMEM(table.shape, jnp.bfloat16),
            pltpu.VMEM(bands.shape, jnp.bfloat16),
            pltpu.VMEM(ones.shape, jnp.bfloat16),
            pltpu.VMEM((blocks, BLOCK, NT), jnp.bfloat16),
            pltpu.VMEM((CHUNKS, blocks, 2, BLOCK, 2 * CHUNK), jnp.bfloat16),
            pltpu.VMEM((peers - 1, CHUNKS, BLOCK, 2 * CHUNK), jnp.bfloat16),
            pltpu.VMEM((peers - 1, CHUNKS, BLOCK, 2 * CHUNK), jnp.bfloat16),
            pltpu.SemaphoreType.DMA((3,)),
            pltpu.SemaphoreType.DMA((blocks,)),
            pltpu.SemaphoreType.DMA((teams - 1, blocks)),
            pltpu.SemaphoreType.DMA((teams - 1, blocks)),
            pltpu.SemaphoreType.DMA((peers - 1, CHUNKS)),
            pltpu.SemaphoreType.DMA((peers - 1, CHUNKS)),
            pltpu.VMEM((2, 8, 128), jnp.int32),
            pltpu.VMEM((2, 8, 128), jnp.int32),
            pltpu.VMEM((blocks, CHUNKS, BLOCK, 2 * CHUNK), jnp.bfloat16),
            pltpu.VMEM((CHUNKS, BLOCK, 2 * CHUNK), jnp.bfloat16),
            pltpu.SemaphoreType.DMA((2,)),
            pltpu.SemaphoreType.DMA((blocks, CHUNKS)),
            pltpu.SemaphoreType.DMA((blocks, CHUNKS)),
            pltpu.SemaphoreType.DMA((CHUNKS,)),
        ],
        compiler_params=pltpu.CompilerParams(
            collective_id=0, has_side_effects=True, vmem_limit_bytes=62 * 1024 * 1024
        ),
        cost_estimate=pl.CostEstimate(
            flops=3_000_000_000, bytes_accessed=6_000_000, transcendentals=0
        ),
    )(raw, table, bands, ones, send_blocks.reshape(peers))
    live = pair_count[:, :, :, None, None, None, None, None] > 0
    return jnp.where(live, result, jnp.bfloat16(0.0))


def solution(mesh):
    return jax.shard_map(
        functools.partial(local, mesh.shape["chan"], mesh.shape["tm"]),
        mesh=mesh,
        in_specs=(P(("groups", "chan"), "tm"), P("chan", "tm", None, None), P("chan", "tm", None)),
        out_specs=P(("groups", "chan"), "tm", None, None, None, None, None, None),
        check_vma=False,
    )
```
